32 devices in a mesh: group: 2 (over x), rows: 16 (over z, y, core).
Axes of the slice: x: 2, y: 2, z: 4, core: 2. Of those that a mesh axis runs over, the one named last changes fastest.
Arguments:
- spectra: float32 [4, 1024, 6144], P('group', 'rows'), parts along dimension 0, may hold values from -6 to 6
- plane: float32 [1024, 6144], P('rows'), may hold values from -6 to 6
- interval_edges: int32 [12, 2], replicated, may hold values from 0 to 128
- tile_shifts: int32 [4, 12, 2], P('group'), parts along dimension 0, may hold values from -8 to 8, as said below
Outputs:
- correlation: float32 [4, 1024, 6144], P('group', 'rows'), parts along dimension 0
- aligned_spectra: float32 [4, 1024, 6144], P('group', 'rows'), parts along dimension 0
The draws below stay inside these ranges and needn't reach their ends.
There are 2 independent parts, one for each index of `group`. The reference program is written for one: setup_inputs(seed, part) draws one part's arguments, and reference() takes and returns one part's arrays. A program takes and returns all parts, laid end to end along the dimension named above; an argument that names none is the same for every part. Nothing has to cross between parts.
Inputs may be any that keep to these rules, and one draw needn't show every extreme that they name: `tile_shifts`: both shifts lie in -8 to 8; the 1024 shift equals 8 for some tile and -8 for another in every draw.
All inputs are finite; a program needn't handle non-finite values.
Results may differ from the reference program's by a relative error of at most 0.000098.
Values sent between devices are 32-bit elements; how exact they have to be, the bound alone decides.
A program may use at most 128 MiB of HBM per device.

```python
import jax
import jax.numpy as jnp
from jax import lax

F1 = 1024
F2 = 6144
TF2 = 512
MAXS = 8
SPEC = 2
T2 = 12


def draw_tile_shifts(key, part):
    first_key, second_key, third_key = jax.random.split(key, 3)
    total = SPEC * T2
    values = jax.random.randint(first_key, (total * 2,), -MAXS, MAXS + 1)
    first_slot = jax.random.randint(second_key, (), 0, total)
    spacing = jax.random.randint(third_key, (), 1, total)
    second_slot = (first_slot + spacing) % total
    values = values.at[2 * first_slot].set(MAXS)
    values = values.at[2 * second_slot].set(-MAXS)
    return values.reshape(SPEC, T2, 2).astype(jnp.int32)


def touch_ends(drawn, stream_key, smallest, high):
    longest = drawn.shape.index(max(drawn.shape))
    spots = []
    for shift in (0, 1):
        where = [jax.random.randint(jax.random.fold_in(stream_key, axis), (), 0, length) for axis, length in enumerate(drawn.shape)]
        where[longest] = (where[longest] + shift) % drawn.shape[longest]
        spots.append(tuple(where))
    return drawn.at[spots[0]].set(smallest).at[spots[1]].set(high)


def level_of(stream_key, extent, cuts, smallest, top_value):
    gain, own = 1.0, jax.random.fold_in(stream_key, 6)
    for position, parts in cuts:
        heights = jnp.exp(jax.random.uniform(jax.random.fold_in(own, position), (parts,), jnp.float32, smallest / len(cuts), top_value / len(cuts)))
        gain = gain * jnp.repeat(heights, extent[position] // parts).reshape([-1 if axis == position else 1 for axis in range(len(extent))])
    return gain


def bell_draw(rng, extent, width, limit, cuts=(), kind=jnp.bfloat16):
    drawn = jax.random.normal(rng, extent, jnp.float32) * width
    if len(cuts) > 0:
        drawn = level_of(rng, extent, cuts, -0.22, 0.18) * drawn
    return jnp.clip(drawn, min=-limit, max=limit).astype(kind)


def setup_inputs(seed: int = 0, part: int = 0) -> dict:
    seeds = jax.random.split(jax.random.key(seed), 5)
    own_keys = jax.random.split(jax.random.fold_in(seeds[4], part), 5)
    return {
        "spectra": bell_draw(own_keys[0], (SPEC, F1, F2), 1.0, 6.0, ((1, 16),), jnp.float32),
        "plane": bell_draw(seeds[1], (F1, F2), 1.0, 6.0, ((0, 16),), jnp.float32),
        "interval_edges": touch_ends(jax.random.randint(seeds[2], (T2, 2), 0, TF2 // 4 + 1), jax.random.fold_in(seeds[2], 1), 0, (TF2 // 4 + 1) - 1).astype(jnp.int32),
        "tile_shifts": draw_tile_shifts(jax.random.fold_in(jax.random.fold_in(seeds[4], part), 71), part),
    }


def interval_keep(interval_edges):
    column = jnp.arange(TF2, dtype=jnp.int32)[None, :]
    inside = (column >= interval_edges[:, 0:1]) & (column < TF2 - interval_edges[:, 1:2])
    return jnp.where(inside, 1.0, 0.0).astype(jnp.float32).reshape(F2)


def reference(spectra, plane, interval_edges, tile_shifts):
    keeper = interval_keep(interval_edges)
    plane_hat = jnp.fft.fft2(plane.reshape(F1, T2, TF2), axes=(0, 2))

    def correlate(single):
        single_hat = jnp.fft.fft2((single * keeper).reshape(F1, T2, TF2), axes=(0, 2))
        result = jnp.real(jnp.fft.ifft2(single_hat * jnp.conj(plane_hat), axes=(0, 2)))
        return (result * (float(F1 * TF2) ** -0.5)).reshape(F1, F2).astype(jnp.float32)

    correlation = lax.map(correlate, spectra)
    padded = jnp.pad(spectra, ((0, 0), (MAXS, MAXS), (MAXS, MAXS)))
    row_start = (MAXS - tile_shifts[:, :, 0]).astype(jnp.int32)
    col_start = (jnp.arange(T2, dtype=jnp.int32)[None, :] * TF2 + MAXS - tile_shifts[:, :, 1]).astype(jnp.int32)

    def cut_one(source, top_index, left_index):
        return lax.dynamic_slice(source, (top_index, left_index), (F1, TF2))

    def cut_spectrum(source, top_row, left_row):
        return jax.vmap(cut_one, in_axes=(None, 0, 0))(source, top_row, left_row)

    pieces = jax.vmap(cut_spectrum)(padded, row_start, col_start)
    aligned_spectra = jnp.transpose(pieces, (0, 2, 1, 3)).reshape(SPEC, F1, F2)
    return correlation, aligned_spectra
```

```python
import math

import jax
import jax.numpy as jnp
import numpy as np
from jax import lax
from jax.experimental import pallas as pl
from jax.experimental.pallas import tpu as pltpu
from jax.sharding import PartitionSpec as P

F1 = 1024
TF2 = 512
HALF = TF2 // 2
MAXS = 8
LANES = 128

exact = lax.Precision.HIGH


def trig(rows, columns, modulus):
    angle = np.outer(np.arange(rows), np.arange(columns)) % modulus * (2.0 * math.pi / modulus)
    return np.cos(angle), np.sin(angle)


def column_table():
    return np.stack(trig(F1, F1, F1)).astype(np.float32)


def row_tables(span):
    groups = HALF // span
    cosine, sine = trig(TF2, HALF, TF2)
    alternate = np.where(np.arange(TF2) % 2 == 0, 1.0, -1.0)
    forward_imag = -sine
    forward_imag[:, 0] = alternate
    forward = np.stack([cosine, forward_imag], axis=1)
    forward = forward.reshape(TF2, 2, groups, span).transpose(0, 2, 1, 3)
    forward = forward.reshape(TF2, groups, 2 * span)
    weights = np.where(np.arange(HALF) == 0, 1.0, 2.0)[None, :]
    inverse_imag = -2.0 * sine
    inverse_imag[:, 0] = alternate
    inverse = np.stack([weights * cosine, inverse_imag], axis=1)
    inverse = inverse.reshape(TF2, 2, groups, span).transpose(2, 1, 3, 0)
    inverse = inverse.reshape(groups, 2 * span, TF2) * float(F1 * TF2) ** (-1.5)
    return forward.astype(np.float32), inverse.astype(np.float32)


def align_kernel(shifts, body, above, below, out, padded):
    spectrum = pl.program_id(0)
    height, breadth = body.shape[1:]
    total = height + 2 * MAXS
    margin = jnp.zeros((total, LANES), jnp.float32)
    padded[:, :LANES] = margin
    padded[:, LANES + breadth :] = margin
    padded[:MAXS, LANES : LANES + breadth] = above[0]
    padded[MAXS : MAXS + height, LANES : LANES + breadth] = body[0]
    padded[MAXS + height :, LANES : LANES + breadth] = below[0]
    window = TF2 + 2 * LANES
    for tile in range(breadth // TF2):
        down = shifts[spectrum, tile, 0]
        right = shifts[spectrum, tile, 1]
        part = padded[:, tile * TF2 : tile * TF2 + window]
        part = pltpu.roll(part, lax.rem(right + window, window), 1)[:, LANES : LANES + TF2]
        part = pltpu.roll(part, lax.rem(down + total, total), 0)
        out[0, :, tile * TF2 : (tile + 1) * TF2] = part[MAXS : MAXS + height]


def aligned(spectra, tile_shifts):
    number, height, breadth = spectra.shape
    count = lax.axis_size("rows")
    head = spectra[:, :MAXS]
    tail = spectra[:, height - MAXS :]
    above = lax.ppermute(tail, "rows", [(i, i + 1) for i in range(count - 1)])
    below = lax.ppermute(head, "rows", [(i + 1, i) for i in range(count - 1)])
    whole = pl.BlockSpec((1, height, breadth), lambda s: (s, 0, 0))
    edge = pl.BlockSpec((1, MAXS, breadth), lambda s: (s, 0, 0))
    return pl.pallas_call(
        align_kernel,
        grid=(number,),
        out_shape=jax.ShapeDtypeStruct(spectra.shape, jnp.float32),
        in_specs=[pl.BlockSpec(memory_space=pltpu.SMEM), whole, edge, edge],
        out_specs=whole,
        scratch_shapes=[pltpu.VMEM((height + 2 * MAXS, breadth + 2 * LANES), jnp.float32)],
        compiler_params=pltpu.CompilerParams(vmem_limit_bytes=24 * 2**20),
        cost_estimate=pl.CostEstimate(
            flops=20 * spectra.size, bytes_accessed=8 * spectra.size, transcendentals=0
        ),
    )(tile_shifts, spectra, above, below)


def per_device(spectra, plane, interval_edges, tile_shifts):
    number, height, breadth = spectra.shape
    count = lax.axis_size("rows")
    tiles = breadth // TF2
    span = math.gcd(breadth // 2 // count, HALF)
    groups = HALF // span
    width = 2 * span
    local = tiles * groups // count
    forward, inverse = row_tables(span)
    columns = column_table()

    point = jnp.arange(TF2, dtype=jnp.int32)[None, :]
    inside = (point >= interval_edges[:, 0:1]) & (point < TF2 - interval_edges[:, 1:2])
    keeper = jnp.where(inside, 1.0, 0.0).astype(jnp.float32).reshape(1, breadth)

    def to_columns(rows):
        blocks = rows.reshape(height, tiles, TF2)
        bins = jnp.einsum("rbn,njl->bjrl", blocks, forward, precision=exact)
        sent = bins.reshape(count, local, height, width)
        return lax.all_to_all(sent, "rows", split_axis=0, concat_axis=0, tiled=True)

    def halves(received):
        pencil = received.transpose(0, 2, 1, 3).reshape(F1, local * width)
        both = jnp.einsum("pkn,nl->pkl", columns, pencil, precision=exact)
        return both.reshape(2, F1, local, 2, span)

    granule = lax.axis_index("rows") * local + jnp.arange(local, dtype=jnp.int32)
    packed = (granule % groups == 0)[:, None] & (jnp.arange(span) == 0)[None, :]

    def spectrum_of(both):
        cosine, sine = both[0], both[1]
        return cosine[:, :, 0] + sine[:, :, 1], cosine[:, :, 1] - sine[:, :, 0]

    plane_halves = halves(to_columns(plane))
    plane_real, plane_imag = spectrum_of(plane_halves)

    def back(received):
        both = halves(received)
        real, imag = spectrum_of(both)
        out_real = real * plane_real + imag * plane_imag
        out_imag = imag * plane_real - real * plane_imag
        cosine, sine = both[0], both[1]
        pc, ps = plane_halves[0], plane_halves[1]
        own_real = cosine * pc + sine * ps
        own_imag = cosine * ps - sine * pc
        first = jnp.stack([out_real, out_imag], axis=2)
        second = jnp.stack([-out_imag, out_real], axis=2)
        mask = packed[None, :, None, :]
        first = jnp.where(mask, own_real, first)
        second = jnp.where(mask, -own_imag, second)
        pair = jnp.stack([first, second]).reshape(2, F1, local * width)
        rows = jnp.einsum("pkn,pnl->kl", columns, pair, precision=exact)
        sent = rows.reshape(count, height, local, width).transpose(0, 2, 1, 3)
        return lax.all_to_all(sent, "rows", split_axis=0, concat_axis=0, tiled=True)

    received = [to_columns(spectra[s] * keeper) for s in range(number)]
    aligned_spectra = aligned(spectra, tile_shifts)
    returned = [back(block) for block in received]

    def to_rows(block):
        bins = block.reshape(tiles, groups, height, width)
        return jnp.einsum("bjrl,jln->rbn", bins, inverse, precision=exact).reshape(height, breadth)

    correlation = jnp.stack([to_rows(block) for block in returned])
    return (correlation, aligned_spectra)


def solution(mesh):
    placed = (P("group", "rows", None), P("rows", None), P(), P("group", None, None))
    return jax.shard_map(
        per_device,
        mesh=mesh,
        in_specs=placed,
        out_specs=(P("group", "rows", None), P("group", "rows", None)),
        check_vma=False,
    )
```

```python
import math

import jax
import jax.numpy as jnp
import numpy as np
from jax import lax
from jax.experimental import pallas as pl
from jax.experimental.pallas import tpu as pltpu
from jax.sharding import PartitionSpec as P

F1 = 1024
TF2 = 512
HALF = TF2 // 2
MAXS = 8
LANES = 128

exact = lax.Precision.HIGH
full = lax.Precision.HIGHEST


def trig(rows, columns, modulus):
    angle = np.outer(np.arange(rows), np.arange(columns)) % modulus * (2.0 * math.pi / modulus)
    return np.cos(angle), np.sin(angle)


def column_table():
    return np.stack(trig(F1, F1, F1)).astype(np.float32)


def row_tables(span):
    groups = HALF // span
    cosine, sine = trig(TF2, HALF, TF2)
    alternate = np.where(np.arange(TF2) % 2 == 0, 1.0, -1.0)
    forward_imag = -sine
    forward_imag[:, 0] = alternate
    forward = np.stack([cosine, forward_imag], axis=1)
    forward = forward.reshape(TF2, 2, groups, span).transpose(0, 2, 1, 3)
    forward = forward.reshape(TF2, groups, 2 * span)
    weights = np.where(np.arange(HALF) == 0, 1.0, 2.0)[None, :]
    inverse_imag = -2.0 * sine
    inverse_imag[:, 0] = alternate
    inverse = np.stack([weights * cosine, inverse_imag], axis=1)
    inverse = inverse.reshape(TF2, 2, groups, span).transpose(2, 1, 3, 0)
    inverse = inverse.reshape(groups, 2 * span, TF2) * float(F1 * TF2) ** (-1.5)
    return forward.astype(np.float32), inverse.astype(np.float32)


def align_kernel(shifts, body, above, below, out, padded):
    spectrum = pl.program_id(0)
    height, breadth = body.shape[1:]
    total = height + 2 * MAXS
    margin = jnp.zeros((total, LANES), jnp.float32)
    padded[:, :LANES] = margin
    padded[:, LANES + breadth :] = margin
    padded[:MAXS, LANES : LANES + breadth] = above[0]
    padded[MAXS : MAXS + height, LANES : LANES + breadth] = body[0]
    padded[MAXS + height :, LANES : LANES + breadth] = below[0]
    window = TF2 + 2 * LANES
    for tile in range(breadth // TF2):
        down = shifts[spectrum, tile, 0]
        right = shifts[spectrum, tile, 1]
        part = padded[:, tile * TF2 : tile * TF2 + window]
        part = pltpu.roll(part, lax.rem(right + window, window), 1)[:, LANES : LANES + TF2]
        part = pltpu.roll(part, lax.rem(down + total, total), 0)
        out[0, :, tile * TF2 : (tile + 1) * TF2] = part[MAXS : MAXS + height]


def aligned(spectra, tile_shifts):
    number, height, breadth = spectra.shape
    count = lax.axis_size("rows")
    head = spectra[:, :MAXS]
    tail = spectra[:, height - MAXS :]
    above = lax.ppermute(tail, "rows", [(i, i + 1) for i in range(count - 1)])
    below = lax.ppermute(head, "rows", [(i + 1, i) for i in range(count - 1)])
    whole = pl.BlockSpec((1, height, breadth), lambda s: (s, 0, 0))
    edge = pl.BlockSpec((1, MAXS, breadth), lambda s: (s, 0, 0))
    return pl.pallas_call(
        align_kernel,
        grid=(number,),
        out_shape=jax.ShapeDtypeStruct(spectra.shape, jnp.float32),
        in_specs=[pl.BlockSpec(memory_space=pltpu.SMEM), whole, edge, edge],
        out_specs=whole,
        scratch_shapes=[pltpu.VMEM((height + 2 * MAXS, breadth + 2 * LANES), jnp.float32)],
        compiler_params=pltpu.CompilerParams(vmem_limit_bytes=24 * 2**20),
        cost_estimate=pl.CostEstimate(
            flops=20 * spectra.size, bytes_accessed=8 * spectra.size, transcendentals=0
        ),
    )(tile_shifts, spectra, above, below)


def per_device(spectra, plane, interval_edges, tile_shifts):
    number, height, breadth = spectra.shape
    count = lax.axis_size("rows")
    tiles = breadth // TF2
    span = math.gcd(breadth // 2 // count, HALF)
    groups = HALF // span
    width = 2 * span
    local = tiles * groups // count
    forward, inverse = row_tables(span)
    columns = column_table()

    point = jnp.arange(TF2, dtype=jnp.int32)[None, :]
    inside = (point >= interval_edges[:, 0:1]) & (point < TF2 - interval_edges[:, 1:2])
    keeper = jnp.where(inside, 1.0, 0.0).astype(jnp.float32).reshape(1, breadth)

    def to_columns(rows):
        held = rows.shape[0]
        blocks = rows.reshape(held, height, tiles, TF2)
        bins = jnp.einsum("srbn,njl->bjsrl", blocks, forward, precision=full)
        sent = bins.reshape(count, local * held, height, width)
        return lax.all_to_all(sent, "rows", split_axis=0, concat_axis=0, tiled=True)

    def halves(received):
        held = received.shape[1] // local
        pencil = received.transpose(0, 2, 1, 3).reshape(F1, local * held * width)
        both = jnp.einsum("pkn,nl->pkl", columns, pencil, precision=exact)
        return both.reshape(2, F1, local, held, 2, span)

    granule = lax.axis_index("rows") * local + jnp.arange(local, dtype=jnp.int32)
    packed = (granule % groups == 0)[:, None] & (jnp.arange(span) == 0)[None, :]

    def spectrum_of(both):
        cosine, sine = both[0], both[1]
        return cosine[:, :, 0] + sine[:, :, 1], cosine[:, :, 1] - sine[:, :, 0]

    masked = spectra * keeper
    leading = halves(to_columns(jnp.stack([plane, masked[0]])))
    trailing = halves(to_columns(masked[1:]))
    plane_halves = leading[:, :, :, 0]
    plane_real, plane_imag = spectrum_of(plane_halves)

    def back(both):
        real, imag = spectrum_of(both)
        out_real = real * plane_real + imag * plane_imag
        out_imag = imag * plane_real - real * plane_imag
        cosine, sine = both[0], both[1]
        pc, ps = plane_halves[0], plane_halves[1]
        own_real = cosine * pc + sine * ps
        own_imag = cosine * ps - sine * pc
        first = jnp.stack([out_real, out_imag], axis=2)
        second = jnp.stack([-out_imag, out_real], axis=2)
        mask = packed[None, :, None, :]
        first = jnp.where(mask, own_real, first)
        second = jnp.where(mask, -own_imag, second)
        pair = jnp.stack([first, second]).reshape(2, F1, local * width)
        rows = jnp.einsum("pkn,pnl->kl", columns, pair, precision=exact)
        sent = rows.reshape(count, height, local, width).transpose(0, 2, 1, 3)
        return lax.all_to_all(sent, "rows", split_axis=0, concat_axis=0, tiled=True)

    aligned_spectra = aligned(spectra, tile_shifts)
    returned = [back(leading[:, :, :, 1])]
    returned += [back(trailing[:, :, :, s]) for s in range(number - 1)]

    def to_rows(block):
        bins = block.reshape(tiles, groups, height, width)
        return jnp.einsum("bjrl,jln->rbn", bins, inverse, precision=full).reshape(height, breadth)

    correlation = jnp.stack([to_rows(block) for block in returned])
    return (correlation, aligned_spectra)


def solution(mesh):
    placed = (P("group", "rows", None), P("rows", None), P(), P("group", None, None))
    return jax.shard_map(
        per_device,
        mesh=mesh,
        in_specs=placed,
        out_specs=(P("group", "rows", None), P("group", "rows", None)),
        check_vma=False,
    )
```

```python
import math

import jax
import jax.numpy as jnp
import numpy as np
from jax import lax
from jax.experimental import pallas as pl
from jax.experimental.pallas import tpu as pltpu
from jax.sharding import PartitionSpec as P

F1 = 1024
TF2 = 512
HALF = TF2 // 2
MAXS = 8
LANES = 128

exact = lax.Precision.HIGH
full = lax.Precision.HIGHEST


def trig(rows, columns, modulus):
    angle = np.outer(np.arange(rows), np.arange(columns)) % modulus * (2.0 * math.pi / modulus)
    return np.cos(angle), np.sin(angle)


def column_table():
    return np.stack(trig(F1, F1, F1))


def row_tables(span):
    groups = HALF // span
    cosine, sine = trig(TF2, HALF, TF2)
    alternate = np.where(np.arange(TF2) % 2 == 0, 1.0, -1.0)
    forward_imag = -sine
    forward_imag[:, 0] = alternate
    forward = np.stack([cosine, forward_imag], axis=1)
    forward = forward.reshape(TF2, 2, groups, span).transpose(0, 2, 1, 3)
    forward = forward.reshape(TF2, groups, 2 * span)
    weights = np.where(np.arange(HALF) == 0, 1.0, 2.0)[None, :]
    inverse_imag = -2.0 * sine
    inverse_imag[:, 0] = alternate
    inverse = np.stack([weights * cosine, inverse_imag], axis=1)
    inverse = inverse.reshape(TF2, 2, groups, span).transpose(2, 1, 3, 0)
    inverse = inverse.reshape(groups, 2 * span, TF2) * float(F1 * TF2) ** (-1.5)
    return forward.astype(np.float32), inverse.astype(np.float32)


def align_kernel(shifts, body, above, below, out, padded):
    spectrum = pl.program_id(0)
    height, breadth = body.shape[1:]
    total = height + 2 * MAXS
    margin = jnp.zeros((total, LANES), jnp.float32)
    padded[:, :LANES] = margin
    padded[:, LANES + breadth :] = margin
    padded[:MAXS, LANES : LANES + breadth] = above[0]
    padded[MAXS : MAXS + height, LANES : LANES + breadth] = body[0]
    padded[MAXS + height :, LANES : LANES + breadth] = below[0]
    window = TF2 + 2 * LANES
    for tile in range(breadth // TF2):
        down = shifts[spectrum, tile, 0]
        right = shifts[spectrum, tile, 1]
        part = padded[:, tile * TF2 : tile * TF2 + window]
        part = pltpu.roll(part, lax.rem(right + window, window), 1)[:, LANES : LANES + TF2]
        part = pltpu.roll(part, lax.rem(down + total, total), 0)
        out[0, :, tile * TF2 : (tile + 1) * TF2] = part[MAXS : MAXS + height]


def aligned(spectra, tile_shifts):
    number, height, breadth = spectra.shape
    count = lax.axis_size("rows")
    head = spectra[:, :MAXS]
    tail = spectra[:, height - MAXS :]
    above = lax.ppermute(tail, "rows", [(i, i + 1) for i in range(count - 1)])
    below = lax.ppermute(head, "rows", [(i + 1, i) for i in range(count - 1)])
    whole = pl.BlockSpec((1, height, breadth), lambda s: (s, 0, 0))
    edge = pl.BlockSpec((1, MAXS, breadth), lambda s: (s, 0, 0))
    return pl.pallas_call(
        align_kernel,
        grid=(number,),
        out_shape=jax.ShapeDtypeStruct(spectra.shape, jnp.float32),
        in_specs=[pl.BlockSpec(memory_space=pltpu.SMEM), whole, edge, edge],
        out_specs=whole,
        scratch_shapes=[pltpu.VMEM((height + 2 * MAXS, breadth + 2 * LANES), jnp.float32)],
        compiler_params=pltpu.CompilerParams(vmem_limit_bytes=24 * 2**20),
        cost_estimate=pl.CostEstimate(
            flops=20 * spectra.size, bytes_accessed=8 * spectra.size, transcendentals=0
        ),
    )(tile_shifts, spectra, above, below)


def plain_products(plane_columns, received, packed):
    count, local, height, width = plane_columns.shape
    span = width // 2
    columns = column_table().astype(np.float32)

    def halves(block):
        pencil = block.transpose(0, 2, 1, 3).reshape(F1, local * width)
        both = jnp.einsum("pkn,nl->pkl", columns, pencil, precision=exact)
        return both.reshape(2, F1, local, 2, span)

    def spectrum_of(both):
        cosine, sine = both[0], both[1]
        return cosine[:, :, 0] + sine[:, :, 1], cosine[:, :, 1] - sine[:, :, 0]

    plane_halves = halves(plane_columns)
    plane_real, plane_imag = spectrum_of(plane_halves)

    def back(block):
        both = halves(block)
        real, imag = spectrum_of(both)
        out_real = real * plane_real + imag * plane_imag
        out_imag = imag * plane_real - real * plane_imag
        cosine, sine = both[0], both[1]
        pc, ps = plane_halves[0], plane_halves[1]
        mask = packed[None, :, None, :]
        first = jnp.stack([out_real, out_imag], axis=2)
        second = jnp.stack([-out_imag, out_real], axis=2)
        first = jnp.where(mask, cosine * pc + sine * ps, first)
        second = jnp.where(mask, sine * pc - cosine * ps, second)
        pair = jnp.stack([first, second]).reshape(2, F1, local * width)
        rows = jnp.einsum("pkn,pnl->kl", columns, pair, precision=exact)
        return rows.reshape(count, height, local, width).transpose(0, 2, 1, 3)

    return [back(block) for block in received]


def split(values):
    high = values.astype(jnp.bfloat16)
    return high, (values - high.astype(jnp.float32)).astype(jnp.bfloat16)


def product_3(table_high, table_low, rows, high, low):
    def dot(a, b):
        return jnp.dot(a, b, preferred_element_type=jnp.float32)

    top = table_high[rows, :]
    return dot(top, high) + (dot(top, low) + dot(table_low[rows, :], high))


CHUNK = 256


def forward_halves(table_high, table_low, block, both, high, low):
    count, local, height, width = block.shape
    for source in range(count):
        for part in range(local):
            rows = slice(source * height, (source + 1) * height)
            lanes = slice(part * width, (part + 1) * width)
            high[rows, lanes], low[rows, lanes] = split(block[source, part])

    @pl.loop(0, 2 * F1 // CHUNK)
    def _(step):
        rows = pl.ds(pl.multiple_of(step * CHUNK, CHUNK), CHUNK)
        both[rows, :] = product_3(table_high, table_low, rows, high[...], low[...])


def product_kernel(
    table_high, table_low, block, plane_both, packed, out, both, high, low, pair_high, pair_low
):
    count, local, height, width = block.shape
    forward_halves(table_high, table_low, block, both, high, low)
    rows_per = 64
    lane = lax.broadcasted_iota(jnp.int32, (rows_per, width), 1)
    is_real = lane < width // 2
    sign = jnp.where(is_real, 1.0, -1.0).astype(jnp.float32)

    def swap(values):
        return pltpu.roll(values, width // 2, 1)

    @pl.loop(0, F1 // rows_per)
    def _(step):
        top = pl.ds(pl.multiple_of(step * rows_per, rows_per), rows_per)
        bottom = pl.ds(pl.multiple_of(F1 + step * rows_per, rows_per), rows_per)
        for part in range(local):
            lanes = slice(part * width, (part + 1) * width)
            c, s = both[top, lanes], both[bottom, lanes]
            pc, ps = plane_both[top, lanes], plane_both[bottom, lanes]
            value = c + sign * swap(s)
            plane_value = pc + sign * swap(ps)
            same = value * plane_value
            cross = swap(value) * plane_value
            product = jnp.where(is_real, same + swap(same), swap(cross) - cross)
            alone = packed[0:1, lanes] > 0.5
            first = jnp.where(alone, c * pc + s * ps, product)
            second = jnp.where(alone, s * pc - c * ps, -sign * swap(product))
            pair_high[top, lanes], pair_low[top, lanes] = split(first)
            pair_high[bottom, lanes], pair_low[bottom, lanes] = split(second)

    per_step = CHUNK // height

    @pl.loop(0, F1 // CHUNK)
    def _(step):
        total = jnp.zeros((CHUNK, local * width), jnp.float32)
        for side in range(2):
            rows = pl.ds(pl.multiple_of(side * F1 + step * CHUNK, CHUNK), CHUNK)
            own = slice(side * F1, (side + 1) * F1)
            total += product_3(table_high, table_low, rows, pair_high[own], pair_low[own])
        for place in range(per_step):
            for part in range(local):
                out[step * per_step + place, part] = total[
                    place * height : (place + 1) * height, part * width : (part + 1) * width
                ]


def kernel_products(plane_columns, received, packed):
    count, local, height, width = plane_columns.shape
    breadth = local * width
    table = column_table().reshape(2 * F1, F1)
    table_high = table.astype(jnp.bfloat16)
    table_low = (table - table_high.astype(np.float64)).astype(jnp.bfloat16)
    lanes = jnp.stack([packed, packed], axis=1).reshape(1, breadth).astype(jnp.float32)
    flops = 12 * F1 * F1 * breadth
    space = pl.BlockSpec(memory_space=pltpu.VMEM)
    params = pltpu.CompilerParams(vmem_limit_bytes=44 * 2**20)
    halves_shape = (2 * F1, breadth)
    scratch = [pltpu.VMEM((F1, breadth), jnp.bfloat16)] * 2
    plane_both = pl.pallas_call(
        forward_halves,
        out_shape=jax.ShapeDtypeStruct(halves_shape, jnp.float32),
        in_specs=[space] * 3,
        out_specs=space,
        scratch_shapes=scratch,
        compiler_params=params,
        cost_estimate=pl.CostEstimate(
            flops=flops, bytes_accessed=8 * F1 * F1, transcendentals=0
        ),
    )(table_high, table_low, plane_columns)
    call = pl.pallas_call(
        product_kernel,
        out_shape=jax.ShapeDtypeStruct(plane_columns.shape, jnp.float32),
        in_specs=[space] * 5,
        out_specs=space,
        scratch_shapes=[pltpu.VMEM(halves_shape, jnp.float32)]
        + scratch
        + [pltpu.VMEM(halves_shape, jnp.bfloat16)] * 2,
        compiler_params=params,
        cost_estimate=pl.CostEstimate(
            flops=2 * flops, bytes_accessed=8 * F1 * F1, transcendentals=0
        ),
    )
    return [call(table_high, table_low, block, plane_both, lanes) for block in received]


def per_device(spectra, plane, interval_edges, tile_shifts):
    number, height, breadth = spectra.shape
    count = lax.axis_size("rows")
    tiles = breadth // TF2
    span = math.gcd(breadth // 2 // count, HALF)
    groups = HALF // span
    width = 2 * span
    local = tiles * groups // count
    forward, inverse = row_tables(span)

    point = jnp.arange(TF2, dtype=jnp.int32)[None, :]
    inside = (point >= interval_edges[:, 0:1]) & (point < TF2 - interval_edges[:, 1:2])
    keeper = jnp.where(inside, 1.0, 0.0).astype(jnp.float32).reshape(1, breadth)

    def to_columns(rows):
        blocks = rows.reshape(height, tiles, TF2)
        bins = jnp.einsum("rbn,njl->bjrl", blocks, forward, precision=full)
        sent = bins.reshape(count, local, height, width)
        return lax.all_to_all(sent, "rows", split_axis=0, concat_axis=0, tiled=True)

    granule = lax.axis_index("rows") * local + jnp.arange(local, dtype=jnp.int32)
    packed = (granule % groups == 0)[:, None] & (jnp.arange(span) == 0)[None, :]
    plane_columns = to_columns(plane)
    received = [to_columns(spectra[s] * keeper) for s in range(number)]
    aligned_spectra = aligned(spectra, tile_shifts)
    if width == LANES and height % 16 == 0:
        products = kernel_products(plane_columns, received, packed)
    else:
        products = plain_products(plane_columns, received, packed)
    returned = [
        lax.all_to_all(block, "rows", split_axis=0, concat_axis=0, tiled=True)
        for block in products
    ]

    def to_rows(block):
        bins = block.reshape(tiles, groups, height, width)
        return jnp.einsum("bjrl,jln->rbn", bins, inverse, precision=full).reshape(height, breadth)

    correlation = jnp.stack([to_rows(block) for block in returned])
    return (correlation, aligned_spectra)


def solution(mesh):
    placed = (P("group", "rows", None), P("rows", None), P(), P("group", None, None))
    return jax.shard_map(
        per_device,
        mesh=mesh,
        in_specs=placed,
        out_specs=(P("group", "rows", None), P("group", "rows", None)),
        check_vma=False,
    )
```

```python
import math

import jax
import jax.numpy as jnp
import numpy as np
from jax import lax
from jax.experimental import pallas as pl
from jax.experimental.pallas import tpu as pltpu
from jax.sharding import PartitionSpec as P

F1 = 1024
TF2 = 512
HALF = TF2 // 2
MAXS = 8
LANES = 128

exact = lax.Precision.HIGH
full = lax.Precision.HIGHEST


def trig(rows, columns, modulus):
    angle = np.outer(np.arange(rows), np.arange(columns)) % modulus * (2.0 * math.pi / modulus)
    return np.cos(angle), np.sin(angle)


def column_table():
    return np.stack(trig(F1, F1, F1))


def row_tables(span):
    groups = HALF // span
    cosine, sine = trig(TF2, HALF, TF2)
    alternate = np.where(np.arange(TF2) % 2 == 0, 1.0, -1.0)
    forward_imag = -sine
    forward_imag[:, 0] = alternate
    forward = np.stack([cosine, forward_imag], axis=1)
    forward = forward.reshape(TF2, 2, groups, span).transpose(0, 2, 1, 3)
    forward = forward.reshape(TF2, groups, 2 * span)
    weights = np.where(np.arange(HALF) == 0, 1.0, 2.0)[None, :]
    inverse_imag = -2.0 * sine
    inverse_imag[:, 0] = alternate
    inverse = np.stack([weights * cosine, inverse_imag], axis=1)
    inverse = inverse.reshape(TF2, 2, groups, span).transpose(2, 1, 3, 0)
    inverse = inverse.reshape(groups, 2 * span, TF2) * float(F1 * TF2) ** (-1.5)
    return forward, inverse


def align_kernel(shifts, body, above, below, out, padded):
    spectrum = pl.program_id(0)
    height, breadth = body.shape[1:]
    total = height + 2 * MAXS
    margin = jnp.zeros((total, LANES), jnp.float32)
    padded[:, :LANES] = margin
    padded[:, LANES + breadth :] = margin
    padded[:MAXS, LANES : LANES + breadth] = above[0]
    padded[MAXS : MAXS + height, LANES : LANES + breadth] = body[0]
    padded[MAXS + height :, LANES : LANES + breadth] = below[0]
    window = TF2 + 2 * LANES
    for tile in range(breadth // TF2):
        down = shifts[spectrum, tile, 0]
        right = shifts[spectrum, tile, 1]
        part = padded[:, tile * TF2 : tile * TF2 + window]
        part = pltpu.roll(part, lax.rem(right + window, window), 1)[:, LANES : LANES + TF2]
        part = pltpu.roll(part, lax.rem(down + total, total), 0)
        out[0, :, tile * TF2 : (tile + 1) * TF2] = part[MAXS : MAXS + height]


def aligned(spectra, tile_shifts):
    number, height, breadth = spectra.shape
    count = lax.axis_size("rows")
    head = spectra[:, :MAXS]
    tail = spectra[:, height - MAXS :]
    above = lax.ppermute(tail, "rows", [(i, i + 1) for i in range(count - 1)])
    below = lax.ppermute(head, "rows", [(i + 1, i) for i in range(count - 1)])
    whole = pl.BlockSpec((1, height, breadth), lambda s: (s, 0, 0))
    edge = pl.BlockSpec((1, MAXS, breadth), lambda s: (s, 0, 0))
    return pl.pallas_call(
        align_kernel,
        grid=(number,),
        out_shape=jax.ShapeDtypeStruct(spectra.shape, jnp.float32),
        in_specs=[pl.BlockSpec(memory_space=pltpu.SMEM), whole, edge, edge],
        out_specs=whole,
        scratch_shapes=[pltpu.VMEM((height + 2 * MAXS, breadth + 2 * LANES), jnp.float32)],
        compiler_params=pltpu.CompilerParams(vmem_limit_bytes=24 * 2**20),
        cost_estimate=pl.CostEstimate(
            flops=20 * spectra.size, bytes_accessed=8 * spectra.size, transcendentals=0
        ),
    )(tile_shifts, spectra, above, below)


def plain_products(plane_columns, received, packed):
    count, local, height, width = plane_columns.shape
    span = width // 2
    columns = column_table().astype(np.float32)

    def halves(block):
        pencil = block.transpose(0, 2, 1, 3).reshape(F1, local * width)
        both = jnp.einsum("pkn,nl->pkl", columns, pencil, precision=exact)
        return both.reshape(2, F1, local, 2, span)

    def spectrum_of(both):
        cosine, sine = both[0], both[1]
        return cosine[:, :, 0] + sine[:, :, 1], cosine[:, :, 1] - sine[:, :, 0]

    plane_halves = halves(plane_columns)
    plane_real, plane_imag = spectrum_of(plane_halves)

    def back(block):
        both = halves(block)
        real, imag = spectrum_of(both)
        out_real = real * plane_real + imag * plane_imag
        out_imag = imag * plane_real - real * plane_imag
        cosine, sine = both[0], both[1]
        pc, ps = plane_halves[0], plane_halves[1]
        mask = packed[None, :, None, :]
        first = jnp.stack([out_real, out_imag], axis=2)
        second = jnp.stack([-out_imag, out_real], axis=2)
        first = jnp.where(mask, cosine * pc + sine * ps, first)
        second = jnp.where(mask, sine * pc - cosine * ps, second)
        pair = jnp.stack([first, second]).reshape(2, F1, local * width)
        rows = jnp.einsum("pkn,pnl->kl", columns, pair, precision=exact)
        return rows.reshape(count, height, local, width).transpose(0, 2, 1, 3)

    return [back(block) for block in received]


def split(values):
    high = values.astype(jnp.bfloat16)
    return high, (values - high.astype(jnp.float32)).astype(jnp.bfloat16)


def product_3(table_high, table_low, rows, high, low):
    def dot(a, b):
        return jnp.dot(a, b, preferred_element_type=jnp.float32)

    top = table_high[rows, :]
    return dot(top, high) + (dot(top, low) + dot(table_low[rows, :], high))


CHUNK = 256


def forward_halves(table_high, table_low, block, both, high, low):
    count, local, height, width = block.shape
    for source in range(count):
        for part in range(local):
            rows = slice(source * height, (source + 1) * height)
            lanes = slice(part * width, (part + 1) * width)
            high[rows, lanes], low[rows, lanes] = split(block[source, part])

    @pl.loop(0, 2 * F1 // CHUNK)
    def _(step):
        rows = pl.ds(pl.multiple_of(step * CHUNK, CHUNK), CHUNK)
        both[rows, :] = product_3(table_high, table_low, rows, high[...], low[...])


def product_kernel(
    table_high, table_low, block, plane_both, packed, out, both, high, low, pair_high, pair_low
):
    count, local, height, width = block.shape
    forward_halves(table_high, table_low, block, both, high, low)
    rows_per = 64
    lane = lax.broadcasted_iota(jnp.int32, (rows_per, width), 1)
    is_real = lane < width // 2
    sign = jnp.where(is_real, 1.0, -1.0).astype(jnp.float32)

    def swap(values):
        return pltpu.roll(values, width // 2, 1)

    @pl.loop(0, F1 // rows_per)
    def _(step):
        top = pl.ds(pl.multiple_of(step * rows_per, rows_per), rows_per)
        bottom = pl.ds(pl.multiple_of(F1 + step * rows_per, rows_per), rows_per)
        for part in range(local):
            lanes = slice(part * width, (part + 1) * width)
            c, s = both[top, lanes], both[bottom, lanes]
            pc, ps = plane_both[top, lanes], plane_both[bottom, lanes]
            value = c + sign * swap(s)
            plane_value = pc + sign * swap(ps)
            same = value * plane_value
            cross = swap(value) * plane_value
            product = jnp.where(is_real, same + swap(same), swap(cross) - cross)
            alone = packed[0:1, lanes] > 0.5
            first = jnp.where(alone, c * pc + s * ps, product)
            second = jnp.where(alone, s * pc - c * ps, -sign * swap(product))
            pair_high[top, lanes], pair_low[top, lanes] = split(first)
            pair_high[bottom, lanes], pair_low[bottom, lanes] = split(second)

    per_step = CHUNK // height

    @pl.loop(0, F1 // CHUNK)
    def _(step):
        total = jnp.zeros((CHUNK, local * width), jnp.float32)
        for side in range(2):
            rows = pl.ds(pl.multiple_of(side * F1 + step * CHUNK, CHUNK), CHUNK)
            own = slice(side * F1, (side + 1) * F1)
            total += product_3(table_high, table_low, rows, pair_high[own], pair_low[own])
        for place in range(per_step):
            for part in range(local):
                out[step * per_step + place, part] = total[
                    place * height : (place + 1) * height, part * width : (part + 1) * width
                ]


def kernel_products(plane_columns, received, packed):
    count, local, height, width = plane_columns.shape
    breadth = local * width
    table = column_table().reshape(2 * F1, F1)
    table_high = table.astype(jnp.bfloat16)
    table_low = (table - table_high.astype(np.float64)).astype(jnp.bfloat16)
    lanes = jnp.stack([packed, packed], axis=1).reshape(1, breadth).astype(jnp.float32)
    flops = 12 * F1 * F1 * breadth
    space = pl.BlockSpec(memory_space=pltpu.VMEM)
    params = pltpu.CompilerParams(vmem_limit_bytes=44 * 2**20)
    halves_shape = (2 * F1, breadth)
    scratch = [pltpu.VMEM((F1, breadth), jnp.bfloat16)] * 2
    plane_both = pl.pallas_call(
        forward_halves,
        out_shape=jax.ShapeDtypeStruct(halves_shape, jnp.float32),
        in_specs=[space] * 3,
        out_specs=space,
        scratch_shapes=scratch,
        compiler_params=params,
        cost_estimate=pl.CostEstimate(
            flops=flops, bytes_accessed=8 * F1 * F1, transcendentals=0
        ),
    )(table_high, table_low, plane_columns)
    call = pl.pallas_call(
        product_kernel,
        out_shape=jax.ShapeDtypeStruct(plane_columns.shape, jnp.float32),
        in_specs=[space] * 5,
        out_specs=space,
        scratch_shapes=[pltpu.VMEM(halves_shape, jnp.float32)]
        + scratch
        + [pltpu.VMEM(halves_shape, jnp.bfloat16)] * 2,
        compiler_params=params,
        cost_estimate=pl.CostEstimate(
            flops=2 * flops, bytes_accessed=8 * F1 * F1, transcendentals=0
        ),
    )
    return [call(table_high, table_low, block, plane_both, lanes) for block in received]


def product_of(values, table_high, table_low):
    high, low = split(values)

    def dot(a, b):
        return jnp.dot(a, b, preferred_element_type=jnp.float32)

    return dot(high, table_high) + (dot(low, table_high) + dot(high, table_low))


def bins_kernel(keeper, rows, table_high, table_low, out):
    bins = product_of(rows[...] * keeper[...], table_high[...], table_low[...])
    for group in range(out.shape[0]):
        out[group] = bins[:, group * LANES : (group + 1) * LANES]


def rows_kernel(*refs):
    blocks, (table_high, table_low, out) = refs[:-3], refs[-3:]
    for spectrum, block in enumerate(blocks):
        bins = jnp.concatenate([block[group] for group in range(block.shape[0])], axis=1)
        out[spectrum] = product_of(bins, table_high[...], table_low[...])


def split_table(table):
    high = table.astype(jnp.bfloat16)
    return high, (table - high.astype(np.float64)).astype(jnp.bfloat16)


def kernel_bins(spectra, index, keeper, table):
    height, breadth = spectra.shape[1:]
    tiles, groups = breadth // TF2, TF2 // LANES
    fixed = pl.BlockSpec((TF2, TF2), lambda b: (0, 0))
    return pl.pallas_call(
        bins_kernel,
        grid=(tiles,),
        out_shape=jax.ShapeDtypeStruct((tiles * groups, height, LANES), jnp.float32),
        in_specs=[
            pl.BlockSpec((1, TF2), lambda b: (0, b)),
            pl.BlockSpec((None, height, TF2), lambda b: (index, 0, b)),
            fixed,
            fixed,
        ],
        out_specs=pl.BlockSpec((groups, height, LANES), lambda b: (b, 0, 0)),
        compiler_params=pltpu.CompilerParams(vmem_limit_bytes=24 * 2**20),
        cost_estimate=pl.CostEstimate(
            flops=6 * height * breadth * TF2, bytes_accessed=8 * height * breadth, transcendentals=0
        ),
    )(keeper, spectra, *split_table(table))


def kernel_rows(blocks, table):
    granules, height = blocks[0].shape[:2]
    groups = TF2 // LANES
    tiles = granules // groups
    number = len(blocks)
    fixed = pl.BlockSpec((TF2, TF2), lambda b: (0, 0))
    return pl.pallas_call(
        rows_kernel,
        grid=(tiles,),
        out_shape=jax.ShapeDtypeStruct((number, height, tiles * TF2), jnp.float32),
        in_specs=[pl.BlockSpec((groups, height, LANES), lambda b: (b, 0, 0))] * number
        + [fixed, fixed],
        out_specs=pl.BlockSpec((number, height, TF2), lambda b: (0, 0, b)),
        compiler_params=pltpu.CompilerParams(vmem_limit_bytes=24 * 2**20),
    )(*blocks, *split_table(table))


def per_device(spectra, plane, interval_edges, tile_shifts):
    number, height, breadth = spectra.shape
    count = lax.axis_size("rows")
    tiles = breadth // TF2
    span = math.gcd(breadth // 2 // count, HALF)
    groups = HALF // span
    width = 2 * span
    local = tiles * groups // count
    forward, inverse = row_tables(span)

    point = jnp.arange(TF2, dtype=jnp.int32)[None, :]
    inside = (point >= interval_edges[:, 0:1]) & (point < TF2 - interval_edges[:, 1:2])
    keeper = jnp.where(inside, 1.0, 0.0).astype(jnp.float32).reshape(1, breadth)

    cohorts = lax.axis_size("group")
    share = height // cohorts
    whole_tiles = width == LANES and share % 16 == 0

    def to_columns(rows, index, kept):
        held = rows.shape[1]
        if whole_tiles:
            bins = kernel_bins(rows, index, kept, forward.reshape(TF2, TF2))
        else:
            blocks = (rows[index] * kept).reshape(held, tiles, TF2)
            table = forward.astype(np.float32)
            bins = jnp.einsum("rbn,njl->bjrl", blocks, table, precision=full)
        sent = bins.reshape(count, local, held, width)
        return lax.all_to_all(sent, "rows", split_axis=0, concat_axis=0, tiled=True)

    granule = lax.axis_index("rows") * local + jnp.arange(local, dtype=jnp.int32)
    packed = (granule % groups == 0)[:, None] & (jnp.arange(span) == 0)[None, :]
    own = lax.axis_index("group")
    plane_rows = lax.dynamic_slice_in_dim(plane, own * share, share, axis=0)
    mine = to_columns(plane_rows[None], 0, jnp.ones_like(keeper))
    if cohorts == 2:
        other = lax.ppermute(mine, "group", [(0, 1), (1, 0)])
        ordered = [jnp.where(own == 0, mine, other), jnp.where(own == 0, other, mine)]
        plane_columns = jnp.concatenate(ordered, axis=2)
    else:
        plane_columns = lax.all_gather(mine, "group", axis=2, tiled=True)
    received = [to_columns(spectra, s, keeper) for s in range(number)]
    aligned_spectra = aligned(spectra, tile_shifts)
    if whole_tiles:
        products = kernel_products(plane_columns, received, packed)
    else:
        products = plain_products(plane_columns, received, packed)
    returned = [
        lax.all_to_all(block, "rows", split_axis=0, concat_axis=0, tiled=True)
        for block in products
    ]

    if whole_tiles:
        blocks = [block.reshape(tiles * groups, height, width) for block in returned]
        return (kernel_rows(blocks, inverse.reshape(TF2, TF2)), aligned_spectra)

    def to_rows(block):
        bins = block.reshape(tiles, groups, height, width)
        table = inverse.astype(np.float32)
        return jnp.einsum("bjrl,jln->rbn", bins, table, precision=full).reshape(height, breadth)

    correlation = jnp.stack([to_rows(block) for block in returned])
    return (correlation, aligned_spectra)


def solution(mesh):
    placed = (P("group", "rows", None), P("rows", None), P(), P("group", None, None))
    return jax.shard_map(
        per_device,
        mesh=mesh,
        in_specs=placed,
        out_specs=(P("group", "rows", None), P("group", "rows", None)),
        check_vma=False,
    )
```

```python
import math

import jax
import jax.numpy as jnp
import numpy as np
from jax import lax
from jax.experimental import pallas as pl
from jax.experimental.pallas import tpu as pltpu
from jax.sharding import PartitionSpec as P

F1 = 1024
TF2 = 512
HALF = TF2 // 2
MAXS = 8
LANES = 128

exact = lax.Precision.HIGH
full = lax.Precision.HIGHEST


def trig(rows, columns, modulus):
    angle = np.outer(np.arange(rows), np.arange(columns)) % modulus * (2.0 * math.pi / modulus)
    return np.cos(angle), np.sin(angle)


def column_table():
    return np.stack(trig(F1, F1, F1))


def row_tables(span):
    groups = HALF // span
    cosine, sine = trig(TF2, HALF, TF2)
    alternate = np.where(np.arange(TF2) % 2 == 0, 1.0, -1.0)
    forward_imag = -sine
    forward_imag[:, 0] = alternate
    forward = np.stack([cosine, forward_imag], axis=1)
    forward = forward.reshape(TF2, 2, groups, span).transpose(0, 2, 1, 3)
    forward = forward.reshape(TF2, groups, 2 * span)
    weights = np.where(np.arange(HALF) == 0, 1.0, 2.0)[None, :]
    inverse_imag = -2.0 * sine
    inverse_imag[:, 0] = alternate
    inverse = np.stack([weights * cosine, inverse_imag], axis=1)
    inverse = inverse.reshape(TF2, 2, groups, span).transpose(2, 1, 3, 0)
    inverse = inverse.reshape(groups, 2 * span, TF2) * float(F1 * TF2) ** (-1.5)
    return forward, inverse


def align_kernel(shifts, body, above, below, out, padded):
    spectrum = pl.program_id(0)
    height, breadth = body.shape[1:]
    total = height + 2 * MAXS
    margin = jnp.zeros((total, LANES), jnp.float32)
    padded[:, :LANES] = margin
    padded[:, LANES + breadth :] = margin
    padded[:MAXS, LANES : LANES + breadth] = above[0]
    padded[MAXS : MAXS + height, LANES : LANES + breadth] = body[0]
    padded[MAXS + height :, LANES : LANES + breadth] = below[0]
    window = TF2 + 2 * LANES
    for tile in range(breadth // TF2):
        down = shifts[spectrum, tile, 0]
        right = shifts[spectrum, tile, 1]
        part = padded[:, tile * TF2 : tile * TF2 + window]
        part = pltpu.roll(part, lax.rem(right + window, window), 1)[:, LANES : LANES + TF2]
        part = pltpu.roll(part, lax.rem(down + total, total), 0)
        out[0, :, tile * TF2 : (tile + 1) * TF2] = part[MAXS : MAXS + height]


def aligned(spectra, tile_shifts):
    number, height, breadth = spectra.shape
    count = lax.axis_size("rows")
    head = spectra[:, :MAXS]
    tail = spectra[:, height - MAXS :]
    above = lax.ppermute(tail, "rows", [(i, i + 1) for i in range(count - 1)])
    below = lax.ppermute(head, "rows", [(i + 1, i) for i in range(count - 1)])
    whole = pl.BlockSpec((1, height, breadth), lambda s: (s, 0, 0))
    edge = pl.BlockSpec((1, MAXS, breadth), lambda s: (s, 0, 0))
    return pl.pallas_call(
        align_kernel,
        grid=(number,),
        out_shape=jax.ShapeDtypeStruct(spectra.shape, jnp.float32),
        in_specs=[pl.BlockSpec(memory_space=pltpu.SMEM), whole, edge, edge],
        out_specs=whole,
        scratch_shapes=[pltpu.VMEM((height + 2 * MAXS, breadth + 2 * LANES), jnp.float32)],
        compiler_params=pltpu.CompilerParams(vmem_limit_bytes=24 * 2**20),
        cost_estimate=pl.CostEstimate(
            flops=20 * spectra.size, bytes_accessed=8 * spectra.size, transcendentals=0
        ),
    )(tile_shifts, spectra, above, below)


def plain_products(plane_columns, received, packed):
    count, local, height, width = plane_columns.shape
    span = width // 2
    columns = column_table().astype(np.float32)

    def halves(block):
        pencil = block.transpose(0, 2, 1, 3).reshape(F1, local * width)
        both = jnp.einsum("pkn,nl->pkl", columns, pencil, precision=exact)
        return both.reshape(2, F1, local, 2, span)

    def spectrum_of(both):
        cosine, sine = both[0], both[1]
        return cosine[:, :, 0] + sine[:, :, 1], cosine[:, :, 1] - sine[:, :, 0]

    plane_halves = halves(plane_columns)
    plane_real, plane_imag = spectrum_of(plane_halves)

    def back(block):
        both = halves(block)
        real, imag = spectrum_of(both)
        out_real = real * plane_real + imag * plane_imag
        out_imag = imag * plane_real - real * plane_imag
        cosine, sine = both[0], both[1]
        pc, ps = plane_halves[0], plane_halves[1]
        mask = packed[None, :, None, :]
        first = jnp.stack([out_real, out_imag], axis=2)
        second = jnp.stack([-out_imag, out_real], axis=2)
        first = jnp.where(mask, cosine * pc + sine * ps, first)
        second = jnp.where(mask, sine * pc - cosine * ps, second)
        pair = jnp.stack([first, second]).reshape(2, F1, local * width)
        rows = jnp.einsum("pkn,pnl->kl", columns, pair, precision=exact)
        return rows.reshape(count, height, local, width).transpose(0, 2, 1, 3)

    return [back(block) for block in received]


def split(values):
    high = values.astype(jnp.bfloat16)
    return high, (values - high.astype(jnp.float32)).astype(jnp.bfloat16)


def product_3(table_high, table_low, rows, high, low):
    def dot(a, b):
        return jnp.dot(a, b, preferred_element_type=jnp.float32)

    top = table_high[rows, :]
    return dot(top, high) + (dot(top, low) + dot(table_low[rows, :], high))


CHUNK = 256


def forward_halves(table_high, table_low, block, both, high, low):
    count, local, height, width = block.shape
    for source in range(count):
        for part in range(local):
            rows = slice(source * height, (source + 1) * height)
            lanes = slice(part * width, (part + 1) * width)
            high[rows, lanes], low[rows, lanes] = split(block[source, part])

    @pl.loop(0, 2 * F1 // CHUNK)
    def _(step):
        rows = pl.ds(pl.multiple_of(step * CHUNK, CHUNK), CHUNK)
        both[rows, :] = product_3(table_high, table_low, rows, high[...], low[...])


def product_kernel(
    table_high, table_low, block, plane_both, packed, out, both, high, low, pair_high, pair_low
):
    count, local, height, width = block.shape
    forward_halves(table_high, table_low, block, both, high, low)
    rows_per = 64
    lane = lax.broadcasted_iota(jnp.int32, (rows_per, width), 1)
    is_real = lane < width // 2
    sign = jnp.where(is_real, 1.0, -1.0).astype(jnp.float32)

    def swap(values):
        return pltpu.roll(values, width // 2, 1)

    @pl.loop(0, F1 // rows_per)
    def _(step):
        top = pl.ds(pl.multiple_of(step * rows_per, rows_per), rows_per)
        bottom = pl.ds(pl.multiple_of(F1 + step * rows_per, rows_per), rows_per)
        for part in range(local):
            lanes = slice(part * width, (part + 1) * width)
            c, s = both[top, lanes], both[bottom, lanes]
            pc, ps = plane_both[top, lanes], plane_both[bottom, lanes]
            value = c + sign * swap(s)
            plane_value = pc + sign * swap(ps)
            same = value * plane_value
            cross = swap(value) * plane_value
            product = jnp.where(is_real, same + swap(same), swap(cross) - cross)
            alone = packed[0:1, lanes] > 0.5
            first = jnp.where(alone, c * pc + s * ps, product)
            second = jnp.where(alone, s * pc - c * ps, -sign * swap(product))
            pair_high[top, lanes], pair_low[top, lanes] = split(first)
            pair_high[bottom, lanes], pair_low[bottom, lanes] = split(second)

    per_step = CHUNK // height

    @pl.loop(0, F1 // CHUNK)
    def _(step):
        total = jnp.zeros((CHUNK, local * width), jnp.float32)
        for side in range(2):
            rows = pl.ds(pl.multiple_of(side * F1 + step * CHUNK, CHUNK), CHUNK)
            own = slice(side * F1, (side + 1) * F1)
            total += product_3(table_high, table_low, rows, pair_high[own], pair_low[own])
        for place in range(per_step):
            for part in range(local):
                out[step * per_step + place, part] = total[
                    place * height : (place + 1) * height, part * width : (part + 1) * width
                ]


def column_parts():
    return split_table(column_table().reshape(2 * F1, F1))


def kernel_plane(plane_columns):
    breadth = plane_columns.shape[1] * plane_columns.shape[3]
    space = pl.BlockSpec(memory_space=pltpu.VMEM)
    return pl.pallas_call(
        forward_halves,
        out_shape=jax.ShapeDtypeStruct((2 * F1, breadth), jnp.float32),
        in_specs=[space] * 3,
        out_specs=space,
        scratch_shapes=[pltpu.VMEM((F1, breadth), jnp.bfloat16)] * 2,
        compiler_params=pltpu.CompilerParams(vmem_limit_bytes=44 * 2**20),
        cost_estimate=pl.CostEstimate(
            flops=12 * F1 * F1 * breadth, bytes_accessed=8 * F1 * F1, transcendentals=0
        ),
    )(*column_parts(), plane_columns)


def kernel_products(plane_both, received, packed):
    breadth = plane_both.shape[1]
    lanes = jnp.stack([packed, packed], axis=1).reshape(1, breadth).astype(jnp.float32)
    space = pl.BlockSpec(memory_space=pltpu.VMEM)
    halves_shape = (2 * F1, breadth)
    call = pl.pallas_call(
        product_kernel,
        out_shape=jax.ShapeDtypeStruct(received[0].shape, jnp.float32),
        in_specs=[space] * 5,
        out_specs=space,
        scratch_shapes=[pltpu.VMEM(halves_shape, jnp.float32)]
        + [pltpu.VMEM((F1, breadth), jnp.bfloat16)] * 2
        + [pltpu.VMEM(halves_shape, jnp.bfloat16)] * 2,
        compiler_params=pltpu.CompilerParams(vmem_limit_bytes=44 * 2**20),
        cost_estimate=pl.CostEstimate(
            flops=24 * F1 * F1 * breadth, bytes_accessed=8 * F1 * F1, transcendentals=0
        ),
    )
    return [call(*column_parts(), block, plane_both, lanes) for block in received]


def product_of(values, table_high, table_low):
    high, low = split(values)

    def dot(a, b):
        return jnp.dot(a, b, preferred_element_type=jnp.float32)

    count = values.shape[0]
    both = dot(jnp.concatenate([high, low], axis=0), table_high)
    return both[:count] + (both[count:] + dot(high, table_low))


def bins_kernel(keeper, rows, table_high, table_low, out):
    height, breadth = rows.shape
    groups = TF2 // LANES
    values = rows[...] * keeper[...]
    tiles = [values[:, start : start + TF2] for start in range(0, breadth, TF2)]
    bins = product_of(jnp.concatenate(tiles, axis=0), table_high[...], table_low[...])
    for tile in range(len(tiles)):
        for group in range(groups):
            out[tile * groups + group] = bins[
                tile * height : (tile + 1) * height, group * LANES : (group + 1) * LANES
            ]


def rows_kernel(*refs):
    blocks, (table_high, table_low, out) = refs[:-3], refs[-3:]
    granules, height = blocks[0].shape[:2]
    groups = TF2 // LANES
    places = [(s, t) for s in range(len(blocks)) for t in range(granules // groups)]
    parts = [
        jnp.concatenate([blocks[s][t * groups + group] for group in range(groups)], axis=1)
        for s, t in places
    ]
    rows = product_of(jnp.concatenate(parts, axis=0), table_high[...], table_low[...])
    for place, (s, t) in enumerate(places):
        out[s, :, t * TF2 : (t + 1) * TF2] = rows[place * height : (place + 1) * height]


def tiles_at_once(tiles):
    return 3 if tiles % 3 == 0 else 2 if tiles % 2 == 0 else 1


def split_table(table):
    high = table.astype(jnp.bfloat16)
    return high, (table - high.astype(np.float64)).astype(jnp.bfloat16)


def kernel_bins(spectra, index, keeper, table):
    height, breadth = spectra.shape[1:]
    tiles, groups = breadth // TF2, TF2 // LANES
    step = tiles_at_once(tiles)
    fixed = pl.BlockSpec((TF2, TF2), lambda b: (0, 0))
    return pl.pallas_call(
        bins_kernel,
        grid=(tiles // step,),
        out_shape=jax.ShapeDtypeStruct((tiles * groups, height, LANES), jnp.float32),
        in_specs=[
            pl.BlockSpec((1, step * TF2), lambda b: (0, b)),
            pl.BlockSpec((None, height, step * TF2), lambda b: (index, 0, b)),
            fixed,
            fixed,
        ],
        out_specs=pl.BlockSpec((step * groups, height, LANES), lambda b: (b, 0, 0)),
        compiler_params=pltpu.CompilerParams(vmem_limit_bytes=24 * 2**20),
        cost_estimate=pl.CostEstimate(
            flops=6 * height * breadth * TF2, bytes_accessed=8 * height * breadth, transcendentals=0
        ),
    )(keeper, spectra, *split_table(table))


def kernel_rows(blocks, table):
    granules, height = blocks[0].shape[:2]
    groups = TF2 // LANES
    tiles = granules // groups
    number = len(blocks)
    step = tiles_at_once(tiles)
    fixed = pl.BlockSpec((TF2, TF2), lambda b: (0, 0))
    return pl.pallas_call(
        rows_kernel,
        grid=(tiles // step,),
        out_shape=jax.ShapeDtypeStruct((number, height, tiles * TF2), jnp.float32),
        in_specs=[pl.BlockSpec((step * groups, height, LANES), lambda b: (b, 0, 0))] * number
        + [fixed, fixed],
        out_specs=pl.BlockSpec((number, height, step * TF2), lambda b: (0, 0, b)),
        compiler_params=pltpu.CompilerParams(vmem_limit_bytes=24 * 2**20),
    )(*blocks, *split_table(table))


def per_device(spectra, plane, interval_edges, tile_shifts):
    number, height, breadth = spectra.shape
    count = lax.axis_size("rows")
    tiles = breadth // TF2
    span = math.gcd(breadth // 2 // count, HALF)
    groups = HALF // span
    width = 2 * span
    local = tiles * groups // count
    forward, inverse = row_tables(span)

    point = jnp.arange(TF2, dtype=jnp.int32)[None, :]
    inside = (point >= interval_edges[:, 0:1]) & (point < TF2 - interval_edges[:, 1:2])
    keeper = jnp.where(inside, 1.0, 0.0).astype(jnp.float32).reshape(1, breadth)

    cohorts = lax.axis_size("group")
    share = height // cohorts
    whole_tiles = width == LANES and share % 16 == 0

    def to_columns(rows, index, kept, after=None):
        held = rows.shape[1]
        if whole_tiles:
            bins = kernel_bins(rows, index, kept, forward.reshape(TF2, TF2))
        else:
            blocks = (rows[index] * kept).reshape(held, tiles, TF2)
            table = forward.astype(np.float32)
            bins = jnp.einsum("rbn,njl->bjrl", blocks, table, precision=full)
        sent = bins.reshape(count, local, held, width)
        if after is not None:
            sent, _ = lax.optimization_barrier((sent, after))
        return lax.all_to_all(sent, "rows", split_axis=0, concat_axis=0, tiled=True)

    granule = lax.axis_index("rows") * local + jnp.arange(local, dtype=jnp.int32)
    packed = (granule % groups == 0)[:, None] & (jnp.arange(span) == 0)[None, :]
    own = lax.axis_index("group")
    plane_rows = lax.dynamic_slice_in_dim(plane, own * share, share, axis=0)
    mine = to_columns(plane_rows[None], 0, jnp.ones_like(keeper))
    if cohorts == 2:
        other = lax.ppermute(mine, "group", [(0, 1), (1, 0)])
        ordered = [jnp.where(own == 0, mine, other), jnp.where(own == 0, other, mine)]
        plane_columns = jnp.concatenate(ordered, axis=2)
    else:
        plane_columns = lax.all_gather(mine, "group", axis=2, tiled=True)
    plane_both = kernel_plane(plane_columns) if whole_tiles else None
    received = [to_columns(spectra, s, keeper, plane_both if s else None) for s in range(number)]
    aligned_spectra = aligned(spectra, tile_shifts)
    if whole_tiles:
        products = kernel_products(plane_both, received, packed)
    else:
        products = plain_products(plane_columns, received, packed)
    returned = [
        lax.all_to_all(block, "rows", split_axis=0, concat_axis=0, tiled=True)
        for block in products
    ]

    if whole_tiles:
        blocks = [block.reshape(tiles * groups, height, width) for block in returned]
        return (kernel_rows(blocks, inverse.reshape(TF2, TF2)), aligned_spectra)

    def to_rows(block):
        bins = block.reshape(tiles, groups, height, width)
        table = inverse.astype(np.float32)
        return jnp.einsum("bjrl,jln->rbn", bins, table, precision=full).reshape(height, breadth)

    correlation = jnp.stack([to_rows(block) for block in returned])
    return (correlation, aligned_spectra)


def solution(mesh):
    placed = (P("group", "rows", None), P("rows", None), P(), P("group", None, None))
    return jax.shard_map(
        per_device,
        mesh=mesh,
        in_specs=placed,
        out_specs=(P("group", "rows", None), P("group", "rows", None)),
        check_vma=False,
    )
```
